32 devices in a mesh: groups: 2 (over y), blk: 4 (over z), chan: 4 (over x, core).
Axes of the slice: x: 2, y: 2, z: 4, core: 2. Of those that a mesh axis runs over, the one named last changes fastest.
Arguments:
- fmap1: bfloat16 [128, 256, 128], P(('groups', 'blk'), 'chan'), parts along dimension 0, may hold values from -6 to 6
- fmap2: bfloat16 [128, 256, 128], P(('groups', 'blk'), 'chan'), parts along dimension 0, may hold values from -6 to 6
- windows: int32 [128, 20], P(('groups', 'blk')), parts along dimension 0, may hold values from 0 to 63, as said below
- live: int32 [128], P(('groups', 'blk')), parts along dimension 0, may hold values from 1 to 20, as said below
- cotangent: bfloat16 [128, 20, 128, 128], P(('groups', 'blk')), parts along dimension 0, may hold values from -6 to 6
Outputs:
- grad_one: float32 [128, 256, 128], P(('groups', 'blk'), 'chan'), parts along dimension 0
- grad_two: float32 [128, 256, 128], P(('groups', 'blk'), 'chan'), parts along dimension 0
The draws below stay inside these ranges and needn't reach their ends.
There are 2 independent parts, one for each index of `groups`. The reference program is written for one: setup_inputs(seed, part) draws one part's arguments, and reference() takes and returns one part's arrays. A program takes and returns all parts, laid end to end along the dimension named above; each array names one. Nothing has to cross between parts.
Inputs may be any that keep to these rules, and one draw needn't show every extreme that they name: `windows`: the ids in one row are distinct; they may name blocks anywhere in the frame. Entries at slots live[b] and beyond are padding and carry no weight. `live`: some block uses all 20 slots.
All inputs are finite; a program needn't handle non-finite values.
Results may differ from the reference program's by a relative error of at most 0.0003.
Values may be sent and summed in bfloat16 or wider, within the bound.
A program may use at most 64 MiB of HBM per device.

```python
import math
import jax
import jax.numpy as jnp
from jax import lax

C = 256
S = 128
W = 20
NB = 64


def draw_windows(key, part):
    flow_key, pick_key = jax.random.split(key, 2)
    region = 4
    region_count = (NB + region - 1) // region
    span = 2 * W
    flows = jax.random.randint(flow_key, (region_count,), -NB, NB + 1)
    block_ids = jnp.arange(NB, dtype=jnp.int32)
    centre = jnp.clip(block_ids + flows[block_ids // region], 0, NB - span)
    centre = centre.at[0].set(0)
    centre = centre.at[NB - 1].set(NB - span)
    keys = jax.random.split(pick_key, NB)
    offsets = jax.vmap(lambda row_key: jax.random.permutation(row_key, span)[:W])(keys)
    has_low = jnp.any(offsets[0] == 0)
    offsets = offsets.at[0, 0].set(jnp.where(has_low, offsets[0, 0], 0))
    has_high = jnp.any(offsets[NB - 1] == span - 1)
    offsets = offsets.at[NB - 1, 0].set(jnp.where(has_high, offsets[NB - 1, 0], span - 1))
    rows = centre[:, None] + offsets
    return rows.astype(jnp.int32)


def draw_live(key, part):
    base_key, top_key, low_key = jax.random.split(key, 3)
    base = jax.random.randint(base_key, (NB,), 1, W + 1)
    top_row = jax.random.randint(top_key, (), 0, NB)
    low_row = (top_row + 1 + jax.random.randint(low_key, (), 0, NB - 1)) % NB
    row_ids = jnp.arange(NB)
    counts = jnp.where(row_ids == top_row, W, jnp.where(row_ids == low_row, 1, base))
    return counts.astype(jnp.int32)


def level_of(own_key, shape, cuts, least, top_value):
    gain, own = 1.0, jax.random.fold_in(own_key, 6)
    for dim, blocks in cuts:
        heights = jnp.exp(jax.random.uniform(jax.random.fold_in(own, dim), (blocks,), jnp.float32, least / len(cuts), top_value / len(cuts)))
        gain = gain * jnp.repeat(heights, shape[dim] // blocks).reshape([-1 if axis == dim else 1 for axis in range(len(shape))])
    return gain


def normal_values(own_key, shape, width, most, cuts=(), kind=jnp.bfloat16):
    values = jax.random.normal(own_key, shape, jnp.float32) * width
    if len(cuts) > 0:
        values = level_of(own_key, shape, cuts, -0.22, 0.18) * values
    return jnp.clip(values, min=-most, max=most).astype(kind)


def setup_inputs(seed: int = 0, part: int = 0) -> dict:
    arg_keys = jax.random.split(jax.random.key(seed), 6)
    own_keys = jax.random.split(jax.random.fold_in(arg_keys[5], part), 6)
    return {
        "fmap1": normal_values(own_keys[0], (NB, C, S), 1.0, 6.0, ((0, 4), (1, 4))),
        "fmap2": normal_values(own_keys[1], (NB, C, S), 1.0, 6.0, ((0, 4), (1, 4))),
        "windows": draw_windows(jax.random.fold_in(jax.random.fold_in(arg_keys[5], part), 71), part),
        "live": draw_live(jax.random.fold_in(jax.random.fold_in(arg_keys[5], part), 71), part),
        "cotangent": normal_values(own_keys[4], (NB, W, S, S), 1.0, 6.0, ((0, 4),)),
    }


def reference(fmap1, fmap2, windows, live, cotangent):
    inv_root = 1.0 / math.sqrt(C)
    slot_ids = jnp.arange(W, dtype=jnp.int32)

    def per_block(accum, per_inputs):
        feat_one, window_ids, live_count, tile = per_inputs
        weight_mask = (slot_ids < live_count).astype(jnp.float32)
        chosen = fmap2[window_ids].astype(jnp.float32) * weight_mask[:, None, None]
        tile_f32 = tile.astype(jnp.float32)
        grad_block = jnp.einsum('wij,wcj->ci', tile_f32, chosen) * inv_root
        contrib = jnp.einsum('wij,ci->wcj', tile_f32, feat_one.astype(jnp.float32)) * (inv_root * weight_mask)[:, None, None]
        accum = accum.at[window_ids].add(contrib)
        return (accum, grad_block)
    zero_grad = jnp.zeros((NB, C, S), jnp.float32)
    grad_two, grad_one = lax.scan(per_block, zero_grad, (fmap1, windows, live, cotangent))
    return (grad_one, grad_two)
```

```python
import functools
import math

import jax
import jax.numpy as jnp
from jax import lax
from jax.experimental import pallas as pl
from jax.experimental.pallas import tpu as pltpu
from jax.sharding import PartitionSpec as P

C = 256
MESH = pl.DeviceIdType.MESH
STEPS = 32767.0
FLOOR = 1e-30


def kernel(n, slots_ref, inverse_ref, f1_hbm, f2_hbm, cot_hbm, one_ref, two_ref,
           f1, cot, terms, held, sums, in_r, in_l, in_scale_r, in_scale_l,
           out_r, out_l, out_scale_r, out_scale_l,
           cot_sem, f1_sem, own_sem, ag_send_r, ag_recv_r, ag_send_l, ag_recv_l,
           rs_send_r, rs_recv_r, rs_send_l, rs_recv_l,
           sc_send_r, sc_recv_r, sc_send_l, sc_recv_l):
    blocks, slots, sites, _ = cot.shape
    channels = f1.shape[1]
    inv_root = 1.0 / math.sqrt(C)
    me = lax.axis_index("blk")
    has_right, has_left = me < n - 1, me > 0
    right, left = {"blk": me + 1}, {"blk": me - 1}

    def cot_copy(b):
        return pltpu.make_async_copy(cot_hbm.at[b], cot.at[b], cot_sem.at[b])

    f1_copy = pltpu.make_async_copy(f1_hbm, f1, f1_sem)
    own_rows = pl.ds(me * blocks, blocks)
    own_copy = pltpu.make_async_copy(f2_hbm, held.at[own_rows], own_sem)
    f1_copy.start()

    @pl.loop(0, blocks)
    def _(b):
        cot_copy(b).start()

    own_copy.start()

    barrier = pltpu.get_barrier_semaphore()

    @pl.when(has_right)
    def _():
        pl.semaphore_signal(barrier, inc=1, device_id=right, device_id_type=MESH)

    @pl.when(has_left)
    def _():
        pl.semaphore_signal(barrier, inc=1, device_id=left, device_id_type=MESH)

    pl.semaphore_wait(barrier, has_right.astype(jnp.int32) + has_left.astype(jnp.int32))

    def gather_copy(src, source, step, send, recv, to):
        rows = pl.ds(source * blocks, blocks)
        return pltpu.make_async_remote_copy(
            src_ref=held.at[rows] if src is None else src,
            dst_ref=held.at[rows],
            send_sem=send.at[step],
            recv_sem=recv.at[step],
            device_id=to,
            device_id_type=MESH,
        )

    @pl.when(has_right)
    def _():
        gather_copy(f2_hbm, me, 0, ag_send_r, ag_recv_r, right).start()

    @pl.when(has_left)
    def _():
        gather_copy(f2_hbm, me, 0, ag_send_l, ag_recv_l, left).start()

    held[n * blocks] = jnp.zeros((channels, sites), held.dtype)
    terms[blocks * slots] = jnp.zeros((channels, sites), jnp.float32)

    f1_copy.wait()
    pair = 2 if slots % 2 == 0 else 1

    @pl.loop(0, blocks)
    def _(b):
        cot_copy(b).wait()
        feat = f1[b]
        for w in range(0, slots, pair):
            tile = jnp.concatenate([cot[b, w + i] for i in range(pair)], axis=1)
            res = jnp.dot(feat, tile, preferred_element_type=jnp.float32)
            for i in range(pair):
                terms[b * slots + w + i] = res[:, i * sites:(i + 1) * sites]

    own_copy.wait()

    def local_sums(chunk):
        @pl.loop(0, blocks)
        def _(k):
            row = chunk * blocks + k
            acc = terms[inverse_ref[row, 0]]
            for b in range(1, blocks):
                acc = acc + terms[inverse_ref[row, b]]
            sums[row] = acc * inv_root

    def chunk_at(j):
        return jnp.where(2 * me < n, n - 1 - j, j)

    def data_copy(d, out, inp, send, recv, to):
        return pltpu.make_async_remote_copy(
            src_ref=out.at[d], dst_ref=inp.at[d], send_sem=send.at[d], recv_sem=recv.at[d],
            device_id=to, device_id_type=MESH)

    def right_copies(d, to):
        return (data_copy(d, out_r, in_r, rs_send_r, rs_recv_r, to),
                data_copy(d, out_scale_r, in_scale_r, sc_send_r, sc_recv_r, to))

    def left_copies(d, to):
        return (data_copy(d, out_l, in_l, rs_send_l, rs_recv_l, to),
                data_copy(d, out_scale_l, in_scale_l, sc_send_l, sc_recv_l, to))

    def encode(d, inp, in_scale, out, out_scale):
        @pl.loop(0, blocks)
        def _(k):
            acc = sums[d * blocks + k]
            if inp is not None:
                acc = acc + inp[d, k].astype(jnp.float32) * in_scale[d, pl.ds(k, 1)]
            most = jnp.maximum(jnp.max(jnp.abs(acc), axis=0, keepdims=True), FLOOR)
            out_scale[d, pl.ds(k, 1)] = most * (1.0 / STEPS)
            coded = jnp.round(acc * (STEPS / most)).astype(jnp.int32)
            out[d, k] = coded.astype(jnp.int16)

    def scatter_step(tau):
        t = tau - me
        d = n - 1 - t

        @pl.when((t >= 0) & (d > me))
        def _():
            @pl.when(has_left)
            def _():
                for c in right_copies(d, left):
                    c.wait_recv()
                encode(d, in_r, in_scale_r, out_r, out_scale_r)

            @pl.when(jnp.logical_not(has_left))
            def _():
                encode(d, None, None, out_r, out_scale_r)

            for c in right_copies(d, right):
                c.start()

        e = tau - (n - 1 - me)

        @pl.when((e >= 0) & (e < me))
        def _():
            @pl.when(has_right)
            def _():
                for c in left_copies(e, right):
                    c.wait_recv()
                encode(e, in_l, in_scale_l, out_l, out_scale_l)

            @pl.when(jnp.logical_not(has_right))
            def _():
                encode(e, None, None, out_l, out_scale_l)

            for c in left_copies(e, left):
                c.start()

    def gather_step(h):
        @pl.when(me - h >= 0)
        def _():
            gather_copy(None, me - h, h - 1, ag_send_r, ag_recv_r, left).wait_recv()

            @pl.when(has_right)
            def _():
                gather_copy(None, me - h, h, ag_send_r, ag_recv_r, right).start()

        @pl.when(me + h <= n - 1)
        def _():
            gather_copy(None, me + h, h - 1, ag_send_l, ag_recv_l, right).wait_recv()

            @pl.when(has_left)
            def _():
                gather_copy(None, me + h, h, ag_send_l, ag_recv_l, left).start()

    def grad_one_block(b):
        picked = jnp.concatenate([held[slots_ref[b, w]] for w in range(slots)], axis=1)
        tile = jnp.concatenate([cot[b, w] for w in range(slots)], axis=1)
        one_ref[b] = lax.dot_general(
            picked, tile, (((1,), (1,)), ((), ())), preferred_element_type=jnp.float32) * inv_root

    complete = jnp.maximum(me, n - 1 - me)
    phases = n - complete

    local_sums(chunk_at(0))
    gather_step(1)
    scatter_step(0)

    @pl.loop(1, n)
    def _(j):
        local_sums(chunk_at(j))

    def ones(h):
        first = (h - complete) * blocks // phases
        last = (h - complete + 1) * blocks // phases

        @pl.when(h >= complete)
        def _():
            @pl.loop(first, last)
            def _(b):
                grad_one_block(b)

    @pl.loop(2, n)
    def _(h):
        gather_step(h)
        scatter_step(h - 1)
        ones(h)

    @pl.when(has_left)
    def _():
        for c in right_copies(me, left):
            c.wait_recv()

        @pl.loop(0, blocks)
        def _(k):
            row = me * blocks + k
            sums[row] = sums[row] + in_r[me, k].astype(jnp.float32) * in_scale_r[me, pl.ds(k, 1)]

    @pl.when(has_right)
    def _():
        for c in left_copies(me, right):
            c.wait_recv()

        @pl.loop(0, blocks)
        def _(k):
            row = me * blocks + k
            sums[row] = sums[row] + in_l[me, k].astype(jnp.float32) * in_scale_l[me, pl.ds(k, 1)]

    two_ref[...] = sums[own_rows]

    @pl.when(has_right)
    def _():
        @pl.loop(0, me + 1)
        def _(h):
            gather_copy(None, me - h, h, ag_send_r, ag_recv_r, right).wait_send()

        @pl.loop(me + 1, n)
        def _(d):
            for c in right_copies(d, right):
                c.wait_send()

    @pl.when(has_left)
    def _():
        @pl.loop(0, n - me)
        def _(h):
            gather_copy(None, me + h, h, ag_send_l, ag_recv_l, left).wait_send()

        @pl.loop(0, me)
        def _(d):
            for c in left_copies(d, left):
                c.wait_send()


def body(fmap1, fmap2, windows, live, cotangent):
    blocks, channels, sites = fmap1.shape
    slots = windows.shape[1]
    n = lax.axis_size("blk")
    rows = n * blocks
    used = jnp.arange(slots, dtype=jnp.int32)[None, :] < live[:, None]
    slot_rows = jnp.where(used, windows, rows)
    pair_ids = jnp.arange(blocks * slots, dtype=jnp.int32).reshape(blocks, slots)
    match = slot_rows[None] == jnp.arange(rows, dtype=jnp.int32)[:, None, None]
    spare = blocks * slots
    inverse = spare + jnp.sum(jnp.where(match, pair_ids[None] - spare, 0), axis=2)

    dma = pltpu.SemaphoreType.DMA
    coded = pltpu.VMEM((n, blocks, channels, sites), jnp.int16)
    scale = pltpu.VMEM((n, blocks, sites), jnp.float32)
    smem = pl.BlockSpec(memory_space=pltpu.SMEM)
    hbm = pl.BlockSpec(memory_space=pl.ANY)
    vmem = pl.BlockSpec(memory_space=pltpu.VMEM)
    shape = jax.ShapeDtypeStruct((blocks, channels, sites), jnp.float32)
    return pl.pallas_call(
        functools.partial(kernel, n),
        out_shape=(shape, shape),
        in_specs=[smem, smem, hbm, hbm, hbm],
        out_specs=(vmem, vmem),
        scratch_shapes=[
            pltpu.VMEM(fmap1.shape, fmap1.dtype),
            pltpu.VMEM(cotangent.shape, cotangent.dtype),
            pltpu.VMEM((spare + 1, channels, sites), jnp.float32),
            pltpu.VMEM((rows + 1, channels, sites), fmap2.dtype),
            pltpu.VMEM((rows, channels, sites), jnp.float32),
            coded, coded, scale, scale, coded, coded, scale, scale,
            dma((blocks,)), dma, dma,
        ] + [dma((n,))] * 12,
        compiler_params=pltpu.CompilerParams(
            collective_id=0, has_side_effects=True, vmem_limit_bytes=56 * 1024 * 1024
        ),
    )(slot_rows, inverse, fmap1, fmap2, cotangent)


def solution(mesh):
    placed = (
        P(("groups", "blk"), "chan", None),
        P(("groups", "blk"), "chan", None),
        P(("groups", "blk"), None),
        P(("groups", "blk")),
        P(("groups", "blk"), None, None, None),
    )
    return jax.shard_map(
        body,
        mesh=mesh,
        in_specs=placed,
        out_specs=(P(("groups", "blk"), "chan", None), P(("groups", "blk"), "chan", None)),
        check_vma=False,
    )
```

```python
import functools
import math

import jax
import jax.numpy as jnp
from jax import lax
from jax.experimental import pallas as pl
from jax.experimental.pallas import tpu as pltpu
from jax.sharding import PartitionSpec as P

C = 256
MESH = pl.DeviceIdType.MESH
STEPS = 32767.0
FLOOR = 1e-30
CUTS = 2


def kernel(n, slots_ref, inverse_ref, f1_hbm, f2_hbm, cot_hbm, one_ref, two_ref,
           f1, cot, terms, held, sums, in_r, in_l, in_scale_r, in_scale_l,
           out_r, out_l, out_scale_r, out_scale_l,
           cot_sem, f1_sem, own_sem, ag_send_r, ag_recv_r, ag_send_l, ag_recv_l,
           rs_send_r, rs_recv_r, rs_send_l, rs_recv_l,
           sc_send_r, sc_recv_r, sc_send_l, sc_recv_l):
    blocks, slots, sites, _ = cot.shape
    channels = f1.shape[1]
    cuts, sub = in_scale_r.shape[1:3]
    inv_root = 1.0 / math.sqrt(C)
    me = lax.axis_index("blk")
    has_right, has_left = me < n - 1, me > 0
    right, left = {"blk": me + 1}, {"blk": me - 1}

    def cot_copy(b):
        return pltpu.make_async_copy(cot_hbm.at[b], cot.at[b], cot_sem.at[b])

    f1_copy = pltpu.make_async_copy(f1_hbm, f1, f1_sem)
    own_rows = pl.ds(me * blocks, blocks)
    own_copy = pltpu.make_async_copy(f2_hbm, held.at[own_rows], own_sem)
    f1_copy.start()

    @pl.loop(0, blocks)
    def _(b):
        cot_copy(b).start()

    own_copy.start()

    barrier = pltpu.get_barrier_semaphore()

    @pl.when(has_right)
    def _():
        pl.semaphore_signal(barrier, inc=1, device_id=right, device_id_type=MESH)

    @pl.when(has_left)
    def _():
        pl.semaphore_signal(barrier, inc=1, device_id=left, device_id_type=MESH)

    pl.semaphore_wait(barrier, has_right.astype(jnp.int32) + has_left.astype(jnp.int32))

    def gather_copy(src, source, step, q, send, recv, to):
        rows = pl.ds(source * blocks + q * sub, sub)
        return pltpu.make_async_remote_copy(
            src_ref=held.at[rows] if src is None else src.at[pl.ds(q * sub, sub)],
            dst_ref=held.at[rows],
            send_sem=send.at[step * cuts + q],
            recv_sem=recv.at[step * cuts + q],
            device_id=to,
            device_id_type=MESH,
        )

    @pl.loop(0, cuts)
    def _(q):
        @pl.when(has_right)
        def _():
            gather_copy(f2_hbm, me, 0, q, ag_send_r, ag_recv_r, right).start()

        @pl.when(has_left)
        def _():
            gather_copy(f2_hbm, me, 0, q, ag_send_l, ag_recv_l, left).start()

    held[n * blocks] = jnp.zeros((channels, sites), held.dtype)
    terms[blocks * slots] = jnp.zeros((channels, sites), jnp.float32)

    f1_copy.wait()
    pair = 2 if slots % 2 == 0 else 1

    @pl.loop(0, blocks)
    def _(b):
        cot_copy(b).wait()
        feat = f1[b]
        for w in range(0, slots, pair):
            tile = jnp.concatenate([cot[b, w + i] for i in range(pair)], axis=1)
            res = jnp.dot(feat, tile, preferred_element_type=jnp.float32)
            for i in range(pair):
                terms[b * slots + w + i] = res[:, i * sites:(i + 1) * sites]

    own_copy.wait()

    def local_sums(chunk):
        @pl.loop(0, blocks)
        def _(k):
            row = chunk * blocks + k
            acc = terms[inverse_ref[row, 0]]
            for b in range(1, blocks):
                acc = acc + terms[inverse_ref[row, b]]
            sums[row] = acc * inv_root

    def chunk_at(j):
        return jnp.where(2 * me < n, n - 1 - j, j)

    def data_copy(d, q, out, inp, send, recv, to):
        rows = pl.ds(q * sub, sub)
        return pltpu.make_async_remote_copy(
            src_ref=out.at[d, rows], dst_ref=inp.at[d, rows],
            send_sem=send.at[d * cuts + q], recv_sem=recv.at[d * cuts + q],
            device_id=to, device_id_type=MESH)

    def scale_copy(d, q, out, inp, send, recv, to):
        return pltpu.make_async_remote_copy(
            src_ref=out.at[d, q], dst_ref=inp.at[d, q],
            send_sem=send.at[d * cuts + q], recv_sem=recv.at[d * cuts + q],
            device_id=to, device_id_type=MESH)

    def right_copies(d, q, to):
        return (data_copy(d, q, out_r, in_r, rs_send_r, rs_recv_r, to),
                scale_copy(d, q, out_scale_r, in_scale_r, sc_send_r, sc_recv_r, to))

    def left_copies(d, q, to):
        return (data_copy(d, q, out_l, in_l, rs_send_l, rs_recv_l, to),
                scale_copy(d, q, out_scale_l, in_scale_l, sc_send_l, sc_recv_l, to))

    def encode(d, q, inp, in_scale, out, out_scale):
        @pl.loop(0, sub)
        def _(i):
            k = q * sub + i
            acc = sums[d * blocks + k]
            if inp is not None:
                acc = acc + inp[d, k].astype(jnp.float32) * in_scale[d, q, pl.ds(i, 1)]
            most = jnp.maximum(jnp.max(jnp.abs(acc), axis=0, keepdims=True), FLOOR)
            out_scale[d, q, pl.ds(i, 1)] = most * (1.0 / STEPS)
            coded = jnp.round(acc * (STEPS / most)).astype(jnp.int32)
            out[d, k] = coded.astype(jnp.int16)

    def scatter_step(tau, q):
        t = tau - me
        d = n - 1 - t

        @pl.when((t >= 0) & (d > me))
        def _():
            @pl.when(has_left)
            def _():
                for c in right_copies(d, q, left):
                    c.wait_recv()
                encode(d, q, in_r, in_scale_r, out_r, out_scale_r)

            @pl.when(jnp.logical_not(has_left))
            def _():
                encode(d, q, None, None, out_r, out_scale_r)

            for c in right_copies(d, q, right):
                c.start()

        e = tau - (n - 1 - me)

        @pl.when((e >= 0) & (e < me))
        def _():
            @pl.when(has_right)
            def _():
                for c in left_copies(e, q, right):
                    c.wait_recv()
                encode(e, q, in_l, in_scale_l, out_l, out_scale_l)

            @pl.when(jnp.logical_not(has_right))
            def _():
                encode(e, q, None, None, out_l, out_scale_l)

            for c in left_copies(e, q, left):
                c.start()

    def gather_step(h, q):
        @pl.when(me - h >= 0)
        def _():
            gather_copy(None, me - h, h - 1, q, ag_send_r, ag_recv_r, left).wait_recv()

            @pl.when(has_right)
            def _():
                gather_copy(None, me - h, h, q, ag_send_r, ag_recv_r, right).start()

        @pl.when(me + h <= n - 1)
        def _():
            gather_copy(None, me + h, h - 1, q, ag_send_l, ag_recv_l, right).wait_recv()

            @pl.when(has_left)
            def _():
                gather_copy(None, me + h, h, q, ag_send_l, ag_recv_l, left).start()

    def grad_one_block(b):
        picked = jnp.concatenate([held[slots_ref[b, w]] for w in range(slots)], axis=1)
        tile = jnp.concatenate([cot[b, w] for w in range(slots)], axis=1)
        one_ref[b] = lax.dot_general(
            picked, tile, (((1,), (1,)), ((), ())), preferred_element_type=jnp.float32) * inv_root

    ready = jnp.maximum(me, n - 1 - me) * cuts + cuts - 1
    pieces = n * cuts - ready
    local_sums(chunk_at(0))

    @pl.loop(0, cuts)
    def _(q):
        gather_step(1, q)
        scatter_step(0, q)

    @pl.loop(1, n)
    def _(j):
        local_sums(chunk_at(j))

    @pl.loop(2 * cuts, n * cuts)
    def _(u):
        h, q = u // cuts, u % cuts
        gather_step(h, q)
        scatter_step(h - 1, q)

        @pl.when(u >= ready)
        def _():
            @pl.loop((u - ready) * blocks // pieces, (u - ready + 1) * blocks // pieces)
            def _(b):
                grad_one_block(b)

    @pl.loop(0, cuts)
    def _(q):
        @pl.when(has_left)
        def _():
            for c in right_copies(me, q, left):
                c.wait_recv()

        @pl.when(has_right)
        def _():
            for c in left_copies(me, q, right):
                c.wait_recv()

        @pl.loop(0, sub)
        def _(i):
            k = q * sub + i
            two_ref[k] = sums[me * blocks + k]

            @pl.when(has_left)
            def _():
                two_ref[k] += in_r[me, k].astype(jnp.float32) * in_scale_r[me, q, pl.ds(i, 1)]

            @pl.when(has_right)
            def _():
                two_ref[k] += in_l[me, k].astype(jnp.float32) * in_scale_l[me, q, pl.ds(i, 1)]

    @pl.loop(0, cuts)
    def _(q):
        @pl.when(has_right)
        def _():
            @pl.loop(0, me + 1)
            def _(h):
                gather_copy(None, me - h, h, q, ag_send_r, ag_recv_r, right).wait_send()

            @pl.loop(me + 1, n)
            def _(d):
                for c in right_copies(d, q, right):
                    c.wait_send()

        @pl.when(has_left)
        def _():
            @pl.loop(0, n - me)
            def _(h):
                gather_copy(None, me + h, h, q, ag_send_l, ag_recv_l, left).wait_send()

            @pl.loop(0, me)
            def _(d):
                for c in left_copies(d, q, left):
                    c.wait_send()


def finish(one_in, two_in, one_out, two_out):
    one_out[...] = one_in[...]
    two_out[...] = two_in[...]


def body(fmap1, fmap2, windows, live, cotangent):
    blocks, channels, sites = fmap1.shape
    slots = windows.shape[1]
    n = lax.axis_size("blk")
    rows = n * blocks
    used = jnp.arange(slots, dtype=jnp.int32)[None, :] < live[:, None]
    slot_rows = jnp.where(used, windows, rows)
    pair_ids = jnp.arange(blocks * slots, dtype=jnp.int32).reshape(blocks, slots)
    match = slot_rows[None] == jnp.arange(rows, dtype=jnp.int32)[:, None, None]
    spare = blocks * slots
    inverse = spare + jnp.sum(jnp.where(match, pair_ids[None] - spare, 0), axis=2)

    dma = pltpu.SemaphoreType.DMA
    coded = pltpu.VMEM((n, blocks, channels, sites), jnp.int16)
    cuts = math.gcd(CUTS, blocks)
    scale = pltpu.VMEM((n, cuts, blocks // cuts, sites), jnp.float32)
    smem = pl.BlockSpec(memory_space=pltpu.SMEM)
    hbm = pl.BlockSpec(memory_space=pl.ANY)
    vmem = pl.BlockSpec(memory_space=pltpu.VMEM)
    shape = jax.ShapeDtypeStruct((blocks, channels, sites), jnp.float32)
    one, two = pl.pallas_call(
        functools.partial(kernel, n),
        out_shape=(shape, shape),
        in_specs=[smem, smem, hbm, hbm, hbm],
        out_specs=(vmem, vmem),
        scratch_shapes=[
            pltpu.VMEM(fmap1.shape, fmap1.dtype),
            pltpu.VMEM(cotangent.shape, cotangent.dtype),
            pltpu.VMEM((spare + 1, channels, sites), jnp.float32),
            pltpu.VMEM((rows + 1, channels, sites), fmap2.dtype),
            pltpu.VMEM((rows, channels, sites), jnp.float32),
            coded, coded, scale, scale, coded, coded, scale, scale,
            dma((blocks,)), dma, dma,
        ] + [dma((n * cuts,))] * 12,
        compiler_params=pltpu.CompilerParams(
            collective_id=0, has_side_effects=True, vmem_limit_bytes=56 * 1024 * 1024
        ),
    )(slot_rows, inverse, fmap1, fmap2, cotangent)
    cuts_out = math.gcd(4, blocks)
    part = pl.BlockSpec((blocks // cuts_out, channels, sites), lambda i: (i, 0, 0))
    return pl.pallas_call(
        finish,
        out_shape=(shape, shape),
        grid=(cuts_out,),
        in_specs=[part, part],
        out_specs=(part, part),
    )(one, two)


def solution(mesh):
    placed = (
        P(("groups", "blk"), "chan", None),
        P(("groups", "blk"), "chan", None),
        P(("groups", "blk"), None),
        P(("groups", "blk")),
        P(("groups", "blk"), None, None, None),
    )
    return jax.shard_map(
        body,
        mesh=mesh,
        in_specs=placed,
        out_specs=(P(("groups", "blk"), "chan", None), P(("groups", "blk"), "chan", None)),
        check_vma=False,
    )
```

```python
import functools
import math

import jax
import jax.numpy as jnp
from jax import lax
from jax.experimental import pallas as pl
from jax.experimental.pallas import tpu as pltpu
from jax.sharding import PartitionSpec as P

C = 256
MESH = pl.DeviceIdType.MESH
STEPS = 32767.0
FLOOR = 1e-30
CUTS = 2


def kernel(n, slots_ref, inverse_ref, f1_hbm, f2_hbm, cot_hbm, one_ref, two_ref,
           f1, cot, terms, held, sums, in_r, in_l, in_scale_r, in_scale_l,
           out_r, out_l, out_scale_r, out_scale_l,
           cot_sem, f1_sem, own_sem, ag_send_r, ag_recv_r, ag_send_l, ag_recv_l,
           rs_send_r, rs_recv_r, rs_send_l, rs_recv_l,
           sc_send_r, sc_recv_r, sc_send_l, sc_recv_l):
    blocks, slots, sites, _ = cot.shape
    channels = f1.shape[1]
    cuts, sub = in_scale_r.shape[1:3]
    inv_root = 1.0 / math.sqrt(C)
    me = lax.axis_index("blk")
    has_right, has_left = me < n - 1, me > 0
    right, left = {"blk": me + 1}, {"blk": me - 1}

    def cot_copy(b):
        return pltpu.make_async_copy(cot_hbm.at[b], cot.at[b], cot_sem.at[b])

    f1_copy = pltpu.make_async_copy(f1_hbm, f1, f1_sem)
    own_rows = pl.ds(me * blocks, blocks)
    own_copy = pltpu.make_async_copy(f2_hbm, held.at[own_rows], own_sem)
    f1_copy.start()

    @pl.loop(0, blocks)
    def _(b):
        cot_copy(b).start()

    own_copy.start()

    barrier = pltpu.get_barrier_semaphore()

    @pl.when(has_right)
    def _():
        pl.semaphore_signal(barrier, inc=1, device_id=right, device_id_type=MESH)

    @pl.when(has_left)
    def _():
        pl.semaphore_signal(barrier, inc=1, device_id=left, device_id_type=MESH)

    pl.semaphore_wait(barrier, has_right.astype(jnp.int32) + has_left.astype(jnp.int32))

    def gather_copy(src, source, step, q, send, recv, to):
        rows = pl.ds(source * blocks + q * sub, sub)
        return pltpu.make_async_remote_copy(
            src_ref=held.at[rows] if src is None else src.at[pl.ds(q * sub, sub)],
            dst_ref=held.at[rows],
            send_sem=send.at[step * cuts + q],
            recv_sem=recv.at[step * cuts + q],
            device_id=to,
            device_id_type=MESH,
        )

    @pl.loop(0, cuts)
    def _(q):
        @pl.when(has_right)
        def _():
            gather_copy(f2_hbm, me, 0, q, ag_send_r, ag_recv_r, right).start()

        @pl.when(has_left)
        def _():
            gather_copy(f2_hbm, me, 0, q, ag_send_l, ag_recv_l, left).start()

    held[n * blocks] = jnp.zeros((channels, sites), held.dtype)
    terms[blocks * slots] = jnp.zeros((channels, sites), jnp.float32)

    f1_copy.wait()
    pair = 2 if slots % 2 == 0 else 1

    @pl.loop(0, blocks)
    def _(b):
        cot_copy(b).wait()
        feat = f1[b]
        for w in range(0, slots, pair):
            tile = jnp.concatenate([cot[b, w + i] for i in range(pair)], axis=1)
            res = jnp.dot(feat, tile, preferred_element_type=jnp.float32)
            for i in range(pair):
                terms[b * slots + w + i] = res[:, i * sites:(i + 1) * sites]

    own_copy.wait()

    def local_sums(chunk):
        @pl.loop(0, blocks)
        def _(k):
            row = chunk * blocks + k
            acc = terms[inverse_ref[row, 0]]
            for b in range(1, blocks):
                acc = acc + terms[inverse_ref[row, b]]
            sums[row] = acc * inv_root

    def chunk_at(j):
        return jnp.where(2 * me < n, n - 1 - j, j)

    def data_copy(d, q, out, inp, send, recv, to):
        rows = pl.ds(q * sub, sub)
        return pltpu.make_async_remote_copy(
            src_ref=out.at[d, rows], dst_ref=inp.at[d, rows],
            send_sem=send.at[d * cuts + q], recv_sem=recv.at[d * cuts + q],
            device_id=to, device_id_type=MESH)

    def scale_copy(d, q, out, inp, send, recv, to):
        return pltpu.make_async_remote_copy(
            src_ref=out.at[d, q], dst_ref=inp.at[d, q],
            send_sem=send.at[d * cuts + q], recv_sem=recv.at[d * cuts + q],
            device_id=to, device_id_type=MESH)

    def right_copies(d, q, to):
        return (data_copy(d, q, out_r, in_r, rs_send_r, rs_recv_r, to),
                scale_copy(d, q, out_scale_r, in_scale_r, sc_send_r, sc_recv_r, to))

    def left_copies(d, q, to):
        return (data_copy(d, q, out_l, in_l, rs_send_l, rs_recv_l, to),
                scale_copy(d, q, out_scale_l, in_scale_l, sc_send_l, sc_recv_l, to))

    def encode(d, q, inp, in_scale, out, out_scale):
        @pl.loop(0, sub)
        def _(i):
            k = q * sub + i
            acc = sums[d * blocks + k]
            if inp is not None:
                acc = acc + inp[d, k].astype(jnp.float32) * in_scale[d, q, pl.ds(i, 1)]
            most = jnp.maximum(jnp.max(jnp.abs(acc), axis=0, keepdims=True), FLOOR)
            out_scale[d, q, pl.ds(i, 1)] = most * (1.0 / STEPS)
            coded = jnp.round(acc * (STEPS / most)).astype(jnp.int32)
            out[d, k] = coded.astype(jnp.int16)

    def scatter_step(tau, q):
        t = tau - me
        d = n - 1 - t

        @pl.when((t >= 0) & (d > me))
        def _():
            @pl.when(has_left)
            def _():
                for c in right_copies(d, q, left):
                    c.wait_recv()
                encode(d, q, in_r, in_scale_r, out_r, out_scale_r)

            @pl.when(jnp.logical_not(has_left))
            def _():
                encode(d, q, None, None, out_r, out_scale_r)

            for c in right_copies(d, q, right):
                c.start()

        e = tau - (n - 1 - me)

        @pl.when((e >= 0) & (e < me))
        def _():
            @pl.when(has_right)
            def _():
                for c in left_copies(e, q, right):
                    c.wait_recv()
                encode(e, q, in_l, in_scale_l, out_l, out_scale_l)

            @pl.when(jnp.logical_not(has_right))
            def _():
                encode(e, q, None, None, out_l, out_scale_l)

            for c in left_copies(e, q, left):
                c.start()

    def gather_step(h, q):
        @pl.when(me - h >= 0)
        def _():
            gather_copy(None, me - h, h - 1, q, ag_send_r, ag_recv_r, left).wait_recv()

            @pl.when(has_right)
            def _():
                gather_copy(None, me - h, h, q, ag_send_r, ag_recv_r, right).start()

        @pl.when(me + h <= n - 1)
        def _():
            gather_copy(None, me + h, h - 1, q, ag_send_l, ag_recv_l, right).wait_recv()

            @pl.when(has_left)
            def _():
                gather_copy(None, me + h, h, q, ag_send_l, ag_recv_l, left).start()

    def grad_one_block(b):
        picked = jnp.concatenate([held[slots_ref[b, w]] for w in range(slots)], axis=1)
        tile = jnp.concatenate([cot[b, w] for w in range(slots)], axis=1)
        one_ref[b] = lax.dot_general(
            picked, tile, (((1,), (1,)), ((), ())), preferred_element_type=jnp.float32) * inv_root

    ready = jnp.maximum(me, n - 1 - me) * cuts + cuts - 1
    pieces = n * cuts - ready
    local_sums(chunk_at(0))

    @pl.loop(0, cuts)
    def _(q):
        gather_step(1, q)
        scatter_step(0, q)

    @pl.loop(1, n)
    def _(j):
        local_sums(chunk_at(j))

    @pl.loop(2 * cuts, n * cuts)
    def _(u):
        h, q = u // cuts, u % cuts
        gather_step(h, q)
        scatter_step(h - 1, q)

        @pl.when(u >= ready)
        def _():
            @pl.loop((u - ready) * blocks // pieces, (u - ready + 1) * blocks // pieces)
            def _(b):
                grad_one_block(b)

    @pl.loop(0, cuts)
    def _(q):
        @pl.when(has_left)
        def _():
            for c in right_copies(me, q, left):
                c.wait_recv()

        @pl.when(has_right)
        def _():
            for c in left_copies(me, q, right):
                c.wait_recv()

        @pl.loop(0, sub)
        def _(i):
            k = q * sub + i
            two_ref[k] = sums[me * blocks + k]

            @pl.when(has_left)
            def _():
                two_ref[k] += in_r[me, k].astype(jnp.float32) * in_scale_r[me, q, pl.ds(i, 1)]

            @pl.when(has_right)
            def _():
                two_ref[k] += in_l[me, k].astype(jnp.float32) * in_scale_l[me, q, pl.ds(i, 1)]

    @pl.loop(0, cuts)
    def _(q):
        @pl.when(has_right)
        def _():
            @pl.loop(0, me + 1)
            def _(h):
                gather_copy(None, me - h, h, q, ag_send_r, ag_recv_r, right).wait_send()

            @pl.loop(me + 1, n)
            def _(d):
                for c in right_copies(d, q, right):
                    c.wait_send()

        @pl.when(has_left)
        def _():
            @pl.loop(0, n - me)
            def _(h):
                gather_copy(None, me + h, h, q, ag_send_l, ag_recv_l, left).wait_send()

            @pl.loop(0, me)
            def _(d):
                for c in left_copies(d, q, left):
                    c.wait_send()


def finish(one_in, two_in, one_out, two_out, held, came, left):
    cuts, rows = came.shape[1], one_in.shape[0] // came.shape[1]

    def copies(i, q):
        part = pl.ds(q * rows, rows)
        source, target = ((one_in, one_out), (two_in, two_out))[i]
        return (pltpu.make_async_copy(source.at[part], held.at[i, part], came.at[i, q]),
                pltpu.make_async_copy(held.at[i, part], target.at[part], left.at[i, q]))

    order = [(i, q) for q in range(cuts) for i in range(2)]
    for i, q in order:
        copies(i, q)[0].start()
    for i, q in order:
        copies(i, q)[0].wait()
        copies(i, q)[1].start()
    for i, q in order:
        copies(i, q)[1].wait()


def body(fmap1, fmap2, windows, live, cotangent):
    blocks, channels, sites = fmap1.shape
    slots = windows.shape[1]
    n = lax.axis_size("blk")
    rows = n * blocks
    used = jnp.arange(slots, dtype=jnp.int32)[None, :] < live[:, None]
    slot_rows = jnp.where(used, windows, rows)
    pair_ids = jnp.arange(blocks * slots, dtype=jnp.int32).reshape(blocks, slots)
    match = slot_rows[None] == jnp.arange(rows, dtype=jnp.int32)[:, None, None]
    spare = blocks * slots
    inverse = spare + jnp.sum(jnp.where(match, pair_ids[None] - spare, 0), axis=2)

    dma = pltpu.SemaphoreType.DMA
    coded = pltpu.VMEM((n, blocks, channels, sites), jnp.int16)
    cuts = math.gcd(CUTS, blocks)
    scale = pltpu.VMEM((n, cuts, blocks // cuts, sites), jnp.float32)
    smem = pl.BlockSpec(memory_space=pltpu.SMEM)
    hbm = pl.BlockSpec(memory_space=pl.ANY)
    vmem = pl.BlockSpec(memory_space=pltpu.VMEM)
    shape = jax.ShapeDtypeStruct((blocks, channels, sites), jnp.float32)
    one, two = pl.pallas_call(
        functools.partial(kernel, n),
        out_shape=(shape, shape),
        in_specs=[smem, smem, hbm, hbm, hbm],
        out_specs=(vmem, vmem),
        scratch_shapes=[
            pltpu.VMEM(fmap1.shape, fmap1.dtype),
            pltpu.VMEM(cotangent.shape, cotangent.dtype),
            pltpu.VMEM((spare + 1, channels, sites), jnp.float32),
            pltpu.VMEM((rows + 1, channels, sites), fmap2.dtype),
            pltpu.VMEM((rows, channels, sites), jnp.float32),
            coded, coded, scale, scale, coded, coded, scale, scale,
            dma((blocks,)), dma, dma,
        ] + [dma((n * cuts,))] * 12,
        compiler_params=pltpu.CompilerParams(
            collective_id=0, has_side_effects=True, vmem_limit_bytes=56 * 1024 * 1024
        ),
    )(slot_rows, inverse, fmap1, fmap2, cotangent)
    cuts_out = math.gcd(4, blocks)
    return pl.pallas_call(
        finish,
        out_shape=(shape, shape),
        in_specs=[hbm, hbm],
        out_specs=(hbm, hbm),
        scratch_shapes=[
            pltpu.VMEM((2, blocks, channels, sites), jnp.float32),
            dma((2, cuts_out)), dma((2, cuts_out)),
        ],
    )(one, two)


def solution(mesh):
    placed = (
        P(("groups", "blk"), "chan", None),
        P(("groups", "blk"), "chan", None),
        P(("groups", "blk"), None),
        P(("groups", "blk")),
        P(("groups", "blk"), None, None, None),
    )
    return jax.shard_map(
        body,
        mesh=mesh,
        in_specs=placed,
        out_specs=(P(("groups", "blk"), "chan", None), P(("groups", "blk"), "chan", None)),
        check_vma=False,
    )
```

```python
import functools
import math

import jax
import jax.numpy as jnp
from jax import lax
from jax.experimental import pallas as pl
from jax.experimental.pallas import tpu as pltpu
from jax.sharding import PartitionSpec as P

C = 256
MESH = pl.DeviceIdType.MESH
STEPS = 32767.0
FLOOR = 1e-30
CUTS = 2


def kernel(n, slots_ref, inverse_ref, f1_hbm, f2_hbm, cot_hbm, one_ref, two_ref,
           f1, cot, terms, held, sums, in_r, in_l, in_scale_r, in_scale_l,
           out_r, out_l, out_scale_r, out_scale_l,
           cot_sem, f1_sem, own_sem, ag_send_r, ag_recv_r, ag_send_l, ag_recv_l,
           rs_send_r, rs_recv_r, rs_send_l, rs_recv_l,
           sc_send_r, sc_recv_r, sc_send_l, sc_recv_l):
    blocks, slots, sites, _ = cot.shape
    channels = f1.shape[1]
    cuts, sub = in_scale_r.shape[1:3]
    inv_root = 1.0 / math.sqrt(C)
    me = lax.axis_index("blk")
    has_right, has_left = me < n - 1, me > 0
    right, left = {"blk": me + 1}, {"blk": me - 1}

    def cot_copy(b):
        return pltpu.make_async_copy(cot_hbm.at[b], cot.at[b], cot_sem.at[b])

    f1_copy = pltpu.make_async_copy(f1_hbm, f1, f1_sem)
    own_rows = pl.ds(me * blocks, blocks)
    own_copy = pltpu.make_async_copy(f2_hbm, held.at[own_rows], own_sem)
    f1_copy.start()

    @pl.loop(0, blocks)
    def _(b):
        cot_copy(b).start()

    own_copy.start()

    barrier = pltpu.get_barrier_semaphore()

    @pl.when(has_right)
    def _():
        pl.semaphore_signal(barrier, inc=1, device_id=right, device_id_type=MESH)

    @pl.when(has_left)
    def _():
        pl.semaphore_signal(barrier, inc=1, device_id=left, device_id_type=MESH)

    pl.semaphore_wait(barrier, has_right.astype(jnp.int32) + has_left.astype(jnp.int32))

    def gather_copy(src, source, step, q, send, recv, to):
        rows = pl.ds(source * blocks + q * sub, sub)
        return pltpu.make_async_remote_copy(
            src_ref=held.at[rows] if src is None else src.at[pl.ds(q * sub, sub)],
            dst_ref=held.at[rows],
            send_sem=send.at[step * cuts + q],
            recv_sem=recv.at[step * cuts + q],
            device_id=to,
            device_id_type=MESH,
        )

    @pl.loop(0, cuts)
    def _(q):
        @pl.when(has_right)
        def _():
            gather_copy(f2_hbm, me, 0, q, ag_send_r, ag_recv_r, right).start()

        @pl.when(has_left)
        def _():
            gather_copy(f2_hbm, me, 0, q, ag_send_l, ag_recv_l, left).start()

    held[n * blocks] = jnp.zeros((channels, sites), held.dtype)
    terms[blocks * slots] = jnp.zeros((channels, sites), jnp.float32)

    f1_copy.wait()
    pair = 2 if slots % 2 == 0 else 1

    @pl.loop(0, blocks)
    def _(b):
        cot_copy(b).wait()
        feat = f1[b]
        for w in range(0, slots, pair):
            tile = jnp.concatenate([cot[b, w + i] for i in range(pair)], axis=1)
            res = jnp.dot(feat, tile, preferred_element_type=jnp.float32)
            for i in range(pair):
                terms[b * slots + w + i] = res[:, i * sites:(i + 1) * sites]

    own_copy.wait()

    def local_sums(chunk):
        @pl.loop(0, blocks)
        def _(k):
            row = chunk * blocks + k
            acc = terms[inverse_ref[row, 0]]
            for b in range(1, blocks):
                acc = acc + terms[inverse_ref[row, b]]
            sums[row] = acc * inv_root

    def chunk_at(j):
        return jnp.where(2 * me < n, n - 1 - j, j)

    def data_copy(d, q, out, inp, send, recv, to):
        rows = pl.ds(q * sub, sub)
        return pltpu.make_async_remote_copy(
            src_ref=out.at[d, rows], dst_ref=inp.at[d, rows],
            send_sem=send.at[d * cuts + q], recv_sem=recv.at[d * cuts + q],
            device_id=to, device_id_type=MESH)

    def scale_copy(d, q, out, inp, send, recv, to):
        return pltpu.make_async_remote_copy(
            src_ref=out.at[d, q], dst_ref=inp.at[d, q],
            send_sem=send.at[d * cuts + q], recv_sem=recv.at[d * cuts + q],
            device_id=to, device_id_type=MESH)

    def right_copies(d, q, to):
        return (scale_copy(d, q, out_scale_r, in_scale_r, sc_send_r, sc_recv_r, to),
                data_copy(d, q, out_r, in_r, rs_send_r, rs_recv_r, to))

    def left_copies(d, q, to):
        return (scale_copy(d, q, out_scale_l, in_scale_l, sc_send_l, sc_recv_l, to),
                data_copy(d, q, out_l, in_l, rs_send_l, rs_recv_l, to))

    def encode(d, q, inp, in_scale, out, out_scale):
        @pl.loop(0, sub)
        def _(i):
            k = q * sub + i
            acc = sums[d * blocks + k]
            if inp is not None:
                acc = acc + inp[d, k].astype(jnp.float32) * in_scale[d, q, pl.ds(i, 1)]
            most = jnp.maximum(jnp.max(jnp.abs(acc), axis=0, keepdims=True), FLOOR)
            out_scale[d, q, pl.ds(i, 1)] = most * (1.0 / STEPS)
            coded = jnp.round(acc * (STEPS / most)).astype(jnp.int32)
            out[d, k] = coded.astype(jnp.int16)

    def scatter_step(tau, q):
        t = tau - me
        d = n - 1 - t

        @pl.when((t >= 0) & (d > me))
        def _():
            @pl.when(has_left)
            def _():
                for c in right_copies(d, q, left):
                    c.wait_recv()
                encode(d, q, in_r, in_scale_r, out_r, out_scale_r)

            @pl.when(jnp.logical_not(has_left))
            def _():
                encode(d, q, None, None, out_r, out_scale_r)

            for c in right_copies(d, q, right):
                c.start()

        e = tau - (n - 1 - me)

        @pl.when((e >= 0) & (e < me))
        def _():
            @pl.when(has_right)
            def _():
                for c in left_copies(e, q, right):
                    c.wait_recv()
                encode(e, q, in_l, in_scale_l, out_l, out_scale_l)

            @pl.when(jnp.logical_not(has_right))
            def _():
                encode(e, q, None, None, out_l, out_scale_l)

            for c in left_copies(e, q, left):
                c.start()

    def gather_step(h, q):
        @pl.when(me - h >= 0)
        def _():
            gather_copy(None, me - h, h - 1, q, ag_send_r, ag_recv_r, left).wait_recv()

            @pl.when(has_right)
            def _():
                gather_copy(None, me - h, h, q, ag_send_r, ag_recv_r, right).start()

        @pl.when(me + h <= n - 1)
        def _():
            gather_copy(None, me + h, h - 1, q, ag_send_l, ag_recv_l, right).wait_recv()

            @pl.when(has_left)
            def _():
                gather_copy(None, me + h, h, q, ag_send_l, ag_recv_l, left).start()

    def grad_one_block(b):
        picked = jnp.concatenate([held[slots_ref[b, w]] for w in range(slots)], axis=1)
        tile = jnp.concatenate([cot[b, w] for w in range(slots)], axis=1)
        one_ref[b] = lax.dot_general(
            picked, tile, (((1,), (1,)), ((), ())), preferred_element_type=jnp.float32) * inv_root

    ready = jnp.maximum(me, n - 1 - me) * cuts + cuts - 1
    pieces = n * cuts - ready
    local_sums(chunk_at(0))

    @pl.loop(0, cuts)
    def _(q):
        gather_step(1, q)
        scatter_step(0, q)

    @pl.loop(1, n)
    def _(j):
        local_sums(chunk_at(j))

    @pl.loop(2 * cuts, n * cuts)
    def _(u):
        h, q = u // cuts, u % cuts
        gather_step(h, q)
        scatter_step(h - 1, q)

        @pl.when(u >= ready)
        def _():
            @pl.loop((u - ready) * blocks // pieces, (u - ready + 1) * blocks // pieces)
            def _(b):
                grad_one_block(b)

    @pl.loop(0, cuts)
    def _(q):
        @pl.when(has_left)
        def _():
            for c in right_copies(me, q, left):
                c.wait_recv()

        @pl.when(has_right)
        def _():
            for c in left_copies(me, q, right):
                c.wait_recv()

        @pl.loop(0, sub)
        def _(i):
            k = q * sub + i
            two_ref[k] = sums[me * blocks + k]

            @pl.when(has_left)
            def _():
                two_ref[k] += in_r[me, k].astype(jnp.float32) * in_scale_r[me, q, pl.ds(i, 1)]

            @pl.when(has_right)
            def _():
                two_ref[k] += in_l[me, k].astype(jnp.float32) * in_scale_l[me, q, pl.ds(i, 1)]

    @pl.loop(0, cuts)
    def _(q):
        @pl.when(has_right)
        def _():
            @pl.loop(0, me + 1)
            def _(h):
                gather_copy(None, me - h, h, q, ag_send_r, ag_recv_r, right).wait_send()

            @pl.loop(me + 1, n)
            def _(d):
                for c in right_copies(d, q, right):
                    c.wait_send()

        @pl.when(has_left)
        def _():
            @pl.loop(0, n - me)
            def _(h):
                gather_copy(None, me + h, h, q, ag_send_l, ag_recv_l, left).wait_send()

            @pl.loop(0, me)
            def _(d):
                for c in left_copies(d, q, left):
                    c.wait_send()


def finish(one_in, two_in, one_out, two_out, held, came, left):
    cuts, rows = came.shape[1], one_in.shape[0] // came.shape[1]

    def copies(i, q):
        part = pl.ds(q * rows, rows)
        source, target = ((one_in, one_out), (two_in, two_out))[i]
        return (pltpu.make_async_copy(source.at[part], held.at[i, part], came.at[i, q]),
                pltpu.make_async_copy(held.at[i, part], target.at[part], left.at[i, q]))

    order = [(i, q) for q in range(cuts) for i in range(2)]
    for i, q in order:
        copies(i, q)[0].start()
    for i, q in order:
        copies(i, q)[0].wait()
        copies(i, q)[1].start()
    for i, q in order:
        copies(i, q)[1].wait()


def body(fmap1, fmap2, windows, live, cotangent):
    blocks, channels, sites = fmap1.shape
    slots = windows.shape[1]
    n = lax.axis_size("blk")
    rows = n * blocks
    used = jnp.arange(slots, dtype=jnp.int32)[None, :] < live[:, None]
    slot_rows = jnp.where(used, windows, rows)
    pair_ids = jnp.arange(blocks * slots, dtype=jnp.int32).reshape(blocks, slots)
    match = slot_rows[None] == jnp.arange(rows, dtype=jnp.int32)[:, None, None]
    spare = blocks * slots
    inverse = spare + jnp.sum(jnp.where(match, pair_ids[None] - spare, 0), axis=2)

    dma = pltpu.SemaphoreType.DMA
    coded = pltpu.VMEM((n, blocks, channels, sites), jnp.int16)
    cuts = math.gcd(CUTS, blocks)
    scale = pltpu.VMEM((n, cuts, blocks // cuts, sites), jnp.float32)
    smem = pl.BlockSpec(memory_space=pltpu.SMEM)
    hbm = pl.BlockSpec(memory_space=pl.ANY)
    vmem = pl.BlockSpec(memory_space=pltpu.VMEM)
    shape = jax.ShapeDtypeStruct((blocks, channels, sites), jnp.float32)
    one, two = pl.pallas_call(
        functools.partial(kernel, n),
        out_shape=(shape, shape),
        in_specs=[smem, smem, hbm, hbm, hbm],
        out_specs=(vmem, vmem),
        scratch_shapes=[
            pltpu.VMEM(fmap1.shape, fmap1.dtype),
            pltpu.VMEM(cotangent.shape, cotangent.dtype),
            pltpu.VMEM((spare + 1, channels, sites), jnp.float32),
            pltpu.VMEM((rows + 1, channels, sites), fmap2.dtype),
            pltpu.VMEM((rows, channels, sites), jnp.float32),
            coded, coded, scale, scale, coded, coded, scale, scale,
            dma((blocks,)), dma, dma,
        ] + [dma((n * cuts,))] * 12,
        compiler_params=pltpu.CompilerParams(
            collective_id=0, has_side_effects=True, vmem_limit_bytes=56 * 1024 * 1024
        ),
    )(slot_rows, inverse, fmap1, fmap2, cotangent)
    cuts_out = math.gcd(4, blocks)
    return pl.pallas_call(
        finish,
        out_shape=(shape, shape),
        in_specs=[hbm, hbm],
        out_specs=(hbm, hbm),
        scratch_shapes=[
            pltpu.VMEM((2, blocks, channels, sites), jnp.float32),
            dma((2, cuts_out)), dma((2, cuts_out)),
        ],
    )(one, two)


def solution(mesh):
    placed = (
        P(("groups", "blk"), "chan", None),
        P(("groups", "blk"), "chan", None),
        P(("groups", "blk"), None),
        P(("groups", "blk")),
        P(("groups", "blk"), None, None, None),
    )
    return jax.shard_map(
        body,
        mesh=mesh,
        in_specs=placed,
        out_specs=(P(("groups", "blk"), "chan", None), P(("groups", "blk"), "chan", None)),
        check_vma=False,
    )
```
